32 devices in a mesh: grp: 2 (over y), prow: 4 (over z), pcol: 4 (over x, core).
Axes of the slice: x: 2, y: 2, z: 4, core: 2. Of those that a mesh axis runs over, the one named last changes fastest.
Arguments:
- eigvecs: float32 [8192, 4096], P(('grp', 'prow'), 'pcol'), parts along dimension 0, may hold values from -6 to 6
- y_panels: float32 [2, 8192, 256], P(None, ('grp', 'prow'), 'pcol'), parts along dimension 1, as said below
- t_factors: float32 [4, 256, 256], P('grp'), parts along dimension 0, as said below
Outputs:
- result: float32 [8192, 4096], P(('grp', 'prow'), 'pcol'), parts along dimension 0
The draws below stay inside these ranges and needn't reach their ends.
There are 2 independent parts, one for each index of `grp`. The reference program is written for one: setup_inputs(seed, part) draws one part's arguments, and reference() takes and returns one part's arrays. A program takes and returns all parts, laid end to end along the dimension named above; each array names one. Nothing has to cross between parts.
Inputs may be any that keep to these rules, and one draw needn't show every extreme that they name: `y_panels`: column j of panel k is zero in rows above k * 256 + j and one in that row; t_factors[k] is upper triangular with diagonal between 0.5 and 1.5. Each t_factors[k] is upper triangular.
All inputs are finite; a program needn't handle non-finite values.
Results may differ from the reference program's by a relative error of at most 0.0001.
Values sent between devices are 32-bit elements; how exact they have to be, the bound alone decides.
A program may use at most 64 MiB of HBM per device.

```python
import jax
import jax.numpy as jnp
from jax import lax

NB = 256
PANELS = 2
NCOLS = 4096
SUPPORT = 4096


def draw_y_panels(key, part):
    inner = jax.random.fold_in(key, 11)
    raw = jax.random.truncated_normal(inner, -4.0, 4.0, (PANELS, SUPPORT, NB), jnp.float32)
    raw = raw / jnp.sqrt(jnp.float32(SUPPORT))
    rowidx = jnp.arange(SUPPORT, dtype=jnp.int32)[None, :, None]
    colidx = jnp.arange(NB, dtype=jnp.int32)[None, None, :]
    panel = jnp.arange(PANELS, dtype=jnp.int32)[:, None, None]
    diagrow = panel * NB + colidx
    ones = jnp.where(rowidx == diagrow, 1.0, 0.0).astype(jnp.float32)
    return jnp.where(rowidx > diagrow, raw, ones).astype(jnp.float32)


def draw_t_factors(key, part):
    first = jax.random.fold_in(key, 21)
    second = jax.random.fold_in(key, 22)
    logs = jax.random.uniform(first, (PANELS, NB), jnp.float32, jnp.log(0.5), jnp.log(1.5))
    upper = jax.random.truncated_normal(second, -4.0, 4.0, (PANELS, NB, NB), jnp.float32)
    upper = upper * 0.5 / jnp.sqrt(jnp.float32(NB))
    rowidx = jnp.arange(NB, dtype=jnp.int32)[:, None]
    colidx = jnp.arange(NB, dtype=jnp.int32)[None, :]
    strict = jnp.where(colidx > rowidx, upper, 0.0)
    diagonal = jnp.exp(logs)[:, :, None] * jnp.where(colidx == rowidx, 1.0, 0.0)[None]
    return (strict + diagonal).astype(jnp.float32)


def level_of(rng, dims, split, least, high):
    def one(position, parts):
        draws = jax.random.uniform(jax.random.fold_in(jax.random.fold_in(rng, 6), position), (parts,), jnp.float32, least / len(split), high / len(split))
        return jnp.repeat(jnp.exp(draws), dims[position] // parts).reshape((-1,) + (1,) * (len(dims) - position - 1))

    factor_of = one(*split[0])
    for cut in split[1:]:
        factor_of = factor_of * one(*cut)
    return factor_of


def noise(rng, shape, spread, bound, split=(), kind=jnp.bfloat16):
    loudness = level_of(rng, shape, split, -0.22, 0.18) if split else 1.0
    result = jax.random.normal(rng, shape, jnp.float32) * spread * loudness
    return jnp.minimum(jnp.maximum(result, -bound), bound).astype(kind)


def setup_inputs(seed: int = 0, part: int = 0) -> dict:
    key_list = jax.random.split(jax.random.key(seed), 4)
    part_splits = jax.random.split(jax.random.fold_in(key_list[3], part), 4)
    eigvecs = noise(part_splits[0], (SUPPORT, NCOLS), 1.0, 6.0, ((0, 4), (1, 4)), jnp.float32)
    y_panels = draw_y_panels(jax.random.fold_in(jax.random.fold_in(key_list[3], part), 71), part)
    t_factors = draw_t_factors(jax.random.fold_in(jax.random.fold_in(key_list[3], part), 71), part)
    return {"eigvecs": eigvecs, "y_panels": y_panels, "t_factors": t_factors}


def reference(eigvecs, y_panels, t_factors):
    highest = lax.Precision.HIGHEST
    current = eigvecs
    for index in reversed(range(PANELS)):
        vectors = y_panels[index]
        sums = jnp.einsum("rc,rk->ck", current, vectors, precision=highest)
        scaled = jnp.einsum("ck,jk->cj", sums, t_factors[index], precision=highest)
        current = current - jnp.einsum("rj,cj->rc", vectors, scaled, precision=highest)
    return current
```

```python
import functools

import jax
import jax.numpy as jnp
from jax import lax
from jax.experimental import pallas as pl
from jax.experimental.pallas import tpu as pltpu
from jax.sharding import PartitionSpec as P

F32 = jnp.float32
BF16 = jnp.bfloat16
BLOCK = 256
SUBS = 2
MESH = pl.DeviceIdType.MESH


def split(x):
    high = x.astype(BF16)
    return high, (x - high.astype(F32)).astype(BF16)


def dot3(ah, al, bh, bl, dims):
    dot = functools.partial(
        lax.dot_general, dimension_numbers=(dims, ((), ())), preferred_element_type=F32
    )
    return dot(ah, bh) + (dot(al, bh) + dot(ah, bl))


def kernel(
    rows, nprow, npcol,
    v_hbm, y_hbm, t_hbm, out_hbm,
    vbuf, vh, vl, ybuf, yt, yth, ytl, tbuf, zh, zl, sbuf, ab, sth, stl,
    v_sem, y_sem, t_sem, out_sem,
    ys_sem, yx_sem, yf_sem, yr_sem,
    in_send, in_recv, outw_send,
):
    npan = y_hbm.shape[0]
    kc = y_hbm.shape[2]
    ncb = vbuf.shape[0]
    nx = npcol // 2
    per_phase = ncb * nx
    units = npan * per_phase
    piece = 2 * kc // SUBS
    cb = vbuf.shape[2]

    grp = lax.axis_index("grp")
    row = lax.axis_index("prow")
    col = lax.axis_index("pcol")
    x, core = col // 2, col % 2
    half = nprow // 2
    lower = row < half
    inner = jnp.where(lower, row + 1, row - 1)
    outer = jnp.where(lower, row - 1, row + 1)
    dist = jnp.where(lower, half - 1 - row, row - half)
    centre = dist == 0
    edge = dist == half - 1
    centre_slot = jnp.where(centre, 1, 0)
    lag_cap = min(
        [per_phase + j * nx - ((nx - 1) * (ncb - 1) + j) - 1 for j in range(ncb - 1)]
        + [(ncb - 1) * nx]
    )
    lag = jnp.minimum(2 + 2 * dist, lag_cap)
    max_lag = min(2 + 2 * (half - 1), lag_cap)

    sibling = (grp, row, x * 2 + 1 - core)

    def across(g):
        return (grp, row, ((x + g) % nx) * 2 + core)

    def v_load(j):
        start = pl.multiple_of(j * cb, cb)
        return pltpu.make_async_copy(v_hbm.at[:, pl.ds(start, cb)], vbuf.at[j], v_sem.at[j])

    def out_store(j):
        start = pl.multiple_of(j * cb, cb)
        return pltpu.make_async_copy(vbuf.at[j], out_hbm.at[:, pl.ds(start, cb)], out_sem.at[j])

    def y_load(p):
        return pltpu.make_async_copy(y_hbm.at[p], ybuf.at[p], y_sem.at[p])

    t_load = pltpu.make_async_copy(t_hbm, tbuf, t_sem)
    for p in reversed(range(npan)):
        y_load(p).start()
    for j in range(ncb):
        v_load(j).start()
    t_load.start()

    barrier = pltpu.get_barrier_semaphore()
    pl.semaphore_signal(barrier, inc=1, device_id=(grp, inner, col), device_id_type=MESH)

    @pl.when(jnp.logical_not(edge))
    def _():
        pl.semaphore_signal(barrier, inc=1, device_id=(grp, outer, col), device_id_type=MESH)

    pl.semaphore_signal(barrier, inc=1, device_id=sibling, device_id_type=MESH)
    for g in range(1, nx):
        pl.semaphore_signal(barrier, inc=1, device_id=across(g), device_id_type=MESH)

    for p in reversed(range(npan)):
        y_load(p).wait()
        yt[p, x, core] = jnp.transpose(ybuf[p])

    pl.semaphore_wait(barrier, jnp.where(edge, 1, 2) + nx)

    def y_copy(p, chip, which, send_sem, target):
        return pltpu.make_async_remote_copy(
            src_ref=yt.at[p, chip, which],
            dst_ref=yt.at[p, chip, which],
            send_sem=send_sem,
            recv_sem=yr_sem.at[p, chip, which],
            device_id=target,
            device_id_type=MESH,
        )

    def y_sib(p):
        return y_copy(p, x, core, ys_sem.at[p], sibling)

    def y_across(p, g):
        return y_copy(p, x, core, yx_sem.at[p, g - 1], across(g))

    def chip_at(g):
        return (x + g) % nx

    def y_forward(p, g):
        return y_copy(p, chip_at(g), core, yf_sem.at[p, g - 1], sibling)

    def y_arrived(p, chip, which):
        y_copy(p, chip, which, ys_sem.at[p], sibling).wait_recv()

    def split_y(p, chip):
        high, low = split(yt[p, chip].reshape(2 * kc, rows))
        yth[p, chip] = high
        ytl[p, chip] = low

    def forward_all(p):
        for g in range(1, nx):
            y_arrived(p, chip_at(g), core)
            y_forward(p, g).start()

    def finish_panel(p):
        for g in range(1, nx):
            y_arrived(p, chip_at(g), 1 - core)
            split_y(p, chip_at(g))
        th, tl = split(tbuf[p])
        z = dot3(
            yth[p].reshape(2 * kc * nx, rows), ytl[p].reshape(2 * kc * nx, rows),
            th, tl, ((0,), (0,)),
        )
        high, low = split(z)
        zh[p] = high
        zl[p] = low

    for p in reversed(range(npan)):
        y_sib(p).start()
        if p == npan - 1:
            for g in range(1, nx):
                y_across(p, g).start()
    t_load.wait()
    y_arrived(npan - 1, x, 1 - core)
    split_y(npan - 1, x)

    def decode(u):
        phase = u // per_phase
        r = u % per_phase
        last = r >= (ncb - 1) * nx
        first = phase == 0
        j = jnp.where(first, jnp.where(last, ncb - 1, r % (ncb - 1)), r // nx)
        g = jnp.where(first, jnp.where(last, r - (ncb - 1) * nx, r // (ncb - 1)), r % nx)
        return phase, npan - 1 - phase, j, g

    def inward(u, s):
        at = pl.ds(s * piece, piece)
        return pltpu.make_async_remote_copy(
            src_ref=sbuf.at[u, at],
            dst_ref=ab.at[centre_slot, u, at],
            send_sem=in_send.at[u, s],
            recv_sem=in_recv.at[centre_slot, u, s],
            device_id=(grp, inner, col),
            device_id_type=MESH,
        )

    def outward(u, s):
        at = pl.ds(s * piece, piece)
        return pltpu.make_async_remote_copy(
            src_ref=ab.at[1, u, at],
            dst_ref=ab.at[1, u, at],
            send_sem=outw_send.at[u, s],
            recv_sem=in_recv.at[1, u, s],
            device_id=(grp, outer, col),
            device_id_type=MESH,
        )

    def arrived(slot, u, s):
        at = pl.ds(s * piece, piece)
        pltpu.make_async_remote_copy(
            src_ref=sbuf.at[u, at],
            dst_ref=ab.at[slot, u, at],
            send_sem=in_send.at[u, s],
            recv_sem=in_recv.at[slot, u, s],
            device_id=(grp, inner, col),
            device_id_type=MESH,
        ).wait_recv()

    begin = max(ncb - 2, 0)

    def step(t, carry):
        for f in range(npan):
            p = npan - 1 - f
            if f == 0:
                forward_at, finish_at = begin, begin + 1
            else:
                base = (f - 1) * per_phase + begin
                send_at, forward_at, finish_at = base + 1, base + 3, base + 4

                @pl.when(t == send_at)
                def _():
                    for g in range(1, nx):
                        y_across(p, g).start()

            @pl.when(t == forward_at)
            def _():
                forward_all(p)

            @pl.when(t == finish_at)
            def _():
                if f > 0:
                    y_arrived(p, x, 1 - core)
                    split_y(p, x)
                finish_panel(p)

        @pl.when(t < units)
        def _():
            u = t
            phase, p, j, g = decode(u)

            @pl.when(jnp.logical_and(phase == 0, g == 0))
            def _():
                v_load(j).wait()
                high, low = split(vbuf[j])
                vh[j] = high
                vl[j] = low

            chip = chip_at(g)
            sbuf[u] = dot3(yth[p, chip], ytl[p, chip], vh[j], vl[j], ((1,), (0,)))
            for s in range(SUBS):
                at = pl.ds(s * piece, piece)

                @pl.when(jnp.logical_not(edge))
                def _():
                    arrived(0, u, s)
                    sbuf[u, at] = sbuf[u, at] + ab[0, u, at]

                inward(u, s).start()

        w = t - lag

        @pl.when(jnp.logical_and(w >= 0, w < units))
        def _():
            phase, p, j, g = decode(w)
            chip = chip_at(g)
            for s in range(SUBS):
                at = pl.ds(s * piece, piece)
                arrived(1, w, s)

                @pl.when(centre)
                def _():
                    ab[1, w, at] = ab[1, w, at] + sbuf[w, at]

                @pl.when(jnp.logical_not(edge))
                def _():
                    outward(w, s).start()

                high, low = split(ab[1, w, at])
                sth[j, chip, at] = high
                stl[j, chip, at] = low

            @pl.when(g == nx - 1)
            def _():
                bh = sth[j].reshape(2 * kc * nx, cb)
                bl = stl[j].reshape(2 * kc * nx, cb)
                for r in range(0, rows, BLOCK):
                    at = pl.ds(r, BLOCK)
                    new = vbuf[j, at] - dot3(zh[p, at], zl[p, at], bh, bl, ((1,), (0,)))
                    vbuf[j, at] = new

                    @pl.when(phase < npan - 1)
                    def _():
                        high, low = split(vbuf[j, at])
                        vh[j, at] = high
                        vl[j, at] = low

                @pl.when(phase == npan - 1)
                def _():
                    out_store(j).start()

        return carry

    lax.fori_loop(0, units + max_lag, step, 0)

    for p in range(npan):
        y_sib(p).wait_send()
        for g in range(1, nx):
            y_across(p, g).wait_send()
            y_forward(p, g).wait_send()

    def drain(u, carry):
        for s in range(SUBS):
            inward(u, s).wait_send()

            @pl.when(jnp.logical_not(edge))
            def _():
                outward(u, s).wait_send()

        return carry

    lax.fori_loop(0, units, drain, 0)
    for j in range(ncb):
        out_store(j).wait()


def per_device(nprow, npcol, eigvecs, y_panels, t_factors):
    rows, cols = eigvecs.shape
    npan, _, kc = y_panels.shape
    cb = BLOCK
    ncb = cols // cb
    nx = npcol // 2
    units = npan * ncb * nx
    dma = pltpu.SemaphoreType.DMA
    any_space = pl.BlockSpec(memory_space=pl.ANY)
    nb = kc * npcol
    return pl.pallas_call(
        functools.partial(kernel, rows, nprow, npcol),
        out_shape=jax.ShapeDtypeStruct((rows, cols), F32),
        in_specs=[any_space] * 3,
        out_specs=any_space,
        scratch_shapes=[
            pltpu.VMEM((ncb, rows, cb), F32),
            pltpu.VMEM((ncb, rows, cb), BF16),
            pltpu.VMEM((ncb, rows, cb), BF16),
            pltpu.VMEM((npan, rows, kc), F32),
            pltpu.VMEM((npan, nx, 2, kc, rows), F32),
            pltpu.VMEM((npan, nx, 2 * kc, rows), BF16),
            pltpu.VMEM((npan, nx, 2 * kc, rows), BF16),
            pltpu.VMEM((npan, nb, nb), F32),
            pltpu.VMEM((npan, rows, nb), BF16),
            pltpu.VMEM((npan, rows, nb), BF16),
            pltpu.VMEM((units, 2 * kc, cb), F32),
            pltpu.VMEM((2, units, 2 * kc, cb), F32),
            pltpu.VMEM((ncb, nx, 2 * kc, cb), BF16),
            pltpu.VMEM((ncb, nx, 2 * kc, cb), BF16),
            dma((ncb,)),
            dma((npan,)),
            dma,
            dma((ncb,)),
            dma((npan,)),
            dma((npan, nx - 1)),
            dma((npan, nx - 1)),
            dma((npan, nx, 2)),
            dma((units, SUBS)),
            dma((2, units, SUBS)),
            dma((units, SUBS)),
        ],
        compiler_params=pltpu.CompilerParams(
            collective_id=0, has_side_effects=True, vmem_limit_bytes=50 * 2**20
        ),
        cost_estimate=pl.CostEstimate(
            flops=2 * 3 * npan * rows * nb * (2 * cols + nb),
            bytes_accessed=8 * rows * cols,
            transcendentals=0,
        ),
    )(eigvecs, y_panels, t_factors)


def solution(mesh):
    return jax.shard_map(
        functools.partial(per_device, mesh.shape["prow"], mesh.shape["pcol"]),
        mesh=mesh,
        in_specs=(
            P(("grp", "prow"), "pcol"),
            P(None, ("grp", "prow"), "pcol"),
            P("grp", None, None),
        ),
        out_specs=P(("grp", "prow"), "pcol"),
        check_vma=False,
    )
```

```python
import functools

import jax
import jax.numpy as jnp
from jax import lax
from jax.experimental import pallas as pl
from jax.experimental.pallas import tpu as pltpu
from jax.sharding import PartitionSpec as P

F32 = jnp.float32
BF16 = jnp.bfloat16
BLOCK = 256
SUBS = 2
LAG = 1
MESH = pl.DeviceIdType.MESH


def split(x):
    high = x.astype(BF16)
    return high, (x - high.astype(F32)).astype(BF16)


def dot3(ah, al, bh, bl, dims):
    dot = functools.partial(
        lax.dot_general, dimension_numbers=(dims, ((), ())), preferred_element_type=F32
    )
    return dot(ah, bh) + (dot(al, bh) + dot(ah, bl))


def kernel(
    rows, nprow, npcol,
    v_hbm, y_hbm, t_hbm, out,
    vbuf, vh, vl, yt, yth, ytl, tbuf, zh, zl, sbuf, ab, sth, stl,
    v_sem, y_sem, t_sem,
    ys_sem, yx_sem, yf_sem, yr_sem,
    in_send, in_recv, outw_send,
):
    npan = y_hbm.shape[0]
    kc = y_hbm.shape[1]
    ncb = vbuf.shape[0]
    nx = npcol // 2
    per_phase = ncb * nx
    units = npan * per_phase
    piece = 2 * kc // SUBS
    cb = vbuf.shape[2]

    grp = lax.axis_index("grp")
    row = lax.axis_index("prow")
    col = lax.axis_index("pcol")
    x, core = col // 2, col % 2
    half = nprow // 2
    lower = row < half
    inner = jnp.where(lower, row + 1, row - 1)
    outer = jnp.where(lower, row - 1, row + 1)
    dist = jnp.where(lower, half - 1 - row, row - half)
    centre = dist == 0
    edge = dist == half - 1
    centre_slot = jnp.where(centre, 1, 0)
    lag_cap = min(
        [per_phase + j * nx - ((nx - 1) * (ncb - 1) + j) - 1 for j in range(ncb - 1)]
        + [(ncb - 1) * nx]
    )
    lag = jnp.minimum(LAG + 3 * dist, lag_cap)
    max_lag = min(LAG + 3 * (half - 1), lag_cap)

    sibling = (grp, row, x * 2 + 1 - core)

    def across(g):
        return (grp, row, ((x + g) % nx) * 2 + core)

    def v_load(j):
        start = pl.multiple_of(j * cb, cb)
        return pltpu.make_async_copy(v_hbm.at[:, pl.ds(start, cb)], vbuf.at[j], v_sem.at[j])

    def y_load(p):
        return pltpu.make_async_copy(y_hbm.at[p], yt.at[p, x, core], y_sem.at[p])

    t_load = pltpu.make_async_copy(t_hbm, tbuf, t_sem)
    for p in reversed(range(npan)):
        y_load(p).start()
    for j in range(ncb):
        v_load(j).start()
    t_load.start()

    barrier = pltpu.get_barrier_semaphore()
    pl.semaphore_signal(barrier, inc=1, device_id=(grp, inner, col), device_id_type=MESH)

    @pl.when(jnp.logical_not(edge))
    def _():
        pl.semaphore_signal(barrier, inc=1, device_id=(grp, outer, col), device_id_type=MESH)

    pl.semaphore_signal(barrier, inc=1, device_id=sibling, device_id_type=MESH)
    for g in range(1, nx):
        pl.semaphore_signal(barrier, inc=1, device_id=across(g), device_id_type=MESH)

    for p in reversed(range(npan)):
        y_load(p).wait()
    pl.semaphore_wait(barrier, jnp.where(edge, 1, 2) + nx)

    def y_copy(p, chip, which, send_sem, target):
        return pltpu.make_async_remote_copy(
            src_ref=yt.at[p, chip, which],
            dst_ref=yt.at[p, chip, which],
            send_sem=send_sem,
            recv_sem=yr_sem.at[p, chip, which],
            device_id=target,
            device_id_type=MESH,
        )

    def y_sib(p):
        return y_copy(p, x, core, ys_sem.at[p], sibling)

    def y_across(p, g):
        return y_copy(p, x, core, yx_sem.at[p, g - 1], across(g))

    def chip_at(g):
        return (x + g) % nx

    def y_forward(p, g):
        return y_copy(p, chip_at(g), core, yf_sem.at[p, g - 1], sibling)

    def y_arrived(p, chip, which):
        y_copy(p, chip, which, ys_sem.at[p], sibling).wait_recv()

    def split_y(p, chip):
        for which in range(2):
            split_half(p, chip, which)

    def split_half(p, chip, which):
        high, low = split(yt[p, chip, which])
        yth[p, chip, which] = high
        ytl[p, chip, which] = low

    def forward_all(p):
        for g in range(1, nx):
            y_arrived(p, chip_at(g), core)
            y_forward(p, g).start()

    def finish_panel(p):
        for g in range(1, nx):
            y_arrived(p, chip_at(g), 1 - core)
            split_y(p, chip_at(g))

    def factor_panel(p):
        th, tl = split(tbuf[p])
        z = dot3(
            yth[p].reshape(2 * kc * nx, rows), ytl[p].reshape(2 * kc * nx, rows),
            th, tl, ((0,), (0,)),
        )
        high, low = split(z)
        zh[p] = high
        zl[p] = low

    for p in reversed(range(npan)):
        y_sib(p).start()
        if p == npan - 1:
            for g in range(1, nx):
                y_across(p, g).start()
    split_half(npan - 1, x, core)

    def decode(u):
        phase = u // per_phase
        r = u % per_phase
        last = r >= (ncb - 1) * nx
        first = phase == 0
        j = jnp.where(first, jnp.where(last, ncb - 1, r % (ncb - 1)), r // nx)
        g = jnp.where(first, jnp.where(last, r - (ncb - 1) * nx, r // (ncb - 1)), r % nx)
        return phase, npan - 1 - phase, j, g

    def inward(u, s):
        at = pl.ds(s * piece, piece)
        return pltpu.make_async_remote_copy(
            src_ref=sbuf.at[u, at],
            dst_ref=ab.at[centre_slot, u, at],
            send_sem=in_send.at[u, s],
            recv_sem=in_recv.at[centre_slot, u, s],
            device_id=(grp, inner, col),
            device_id_type=MESH,
        )

    def outward(u, s):
        at = pl.ds(s * piece, piece)
        return pltpu.make_async_remote_copy(
            src_ref=ab.at[1, u, at],
            dst_ref=ab.at[1, u, at],
            send_sem=outw_send.at[u, s],
            recv_sem=in_recv.at[1, u, s],
            device_id=(grp, outer, col),
            device_id_type=MESH,
        )

    def arrived(slot, u, s):
        at = pl.ds(s * piece, piece)
        pltpu.make_async_remote_copy(
            src_ref=sbuf.at[u, at],
            dst_ref=ab.at[slot, u, at],
            send_sem=in_send.at[u, s],
            recv_sem=in_recv.at[slot, u, s],
            device_id=(grp, inner, col),
            device_id_type=MESH,
        ).wait_recv()

    def pass_inward(u, s):
        at = pl.ds(pl.multiple_of(s * piece, piece), piece)

        @pl.when(jnp.logical_not(edge))
        def _():
            arrived(0, u, s)
            sbuf[u, at] = sbuf[u, at] + ab[0, u, at]

        inward(u, s).start()

    begin = max(ncb - 2, 0)

    def step(t, carry):
        for f in range(npan):
            p = npan - 1 - f
            if f == 0:
                finish_at = begin + 1
            else:
                base = (f - 1) * per_phase + begin
                send_at, finish_at = base + 1, base + 4

                @pl.when(t == send_at)
                def _():
                    for g in range(1, nx):
                        y_across(p, g).start()

            @pl.when(t == finish_at)
            def _():
                if f > 0:
                    y_arrived(p, x, 1 - core)
                    split_y(p, x)
                finish_panel(p)

        @pl.when(t < units)
        def _():
            u = t
            phase, p, j, g = decode(u)

            @pl.when(jnp.logical_and(phase == 0, g == 0))
            def _():
                v_load(j).wait()
                high, low = split(vbuf[j])
                vh[j] = high
                vl[j] = low

            chip = chip_at(g)

            @pl.when(t == 0)
            def _():
                for turn, which in enumerate((core, 1 - core)):
                    if turn == 1:
                        y_arrived(p, x, which)
                        split_half(p, x, which)
                    sbuf[u, pl.ds(which * kc, kc)] = dot3(
                        yth[p, chip, which], ytl[p, chip, which], vh[j], vl[j], ((1,), (0,))
                    )
                    pass_inward(u, which)

            @pl.when(t > 0)
            def _():
                sbuf[u] = dot3(
                    yth[p, chip].reshape(2 * kc, rows), ytl[p, chip].reshape(2 * kc, rows),
                    vh[j], vl[j], ((1,), (0,)),
                )
                for s in range(SUBS):
                    pass_inward(u, s)

        for f in range(npan):
            base = max(f - 1, 0) * per_phase + begin

            @pl.when(t == base + (0 if f == 0 else 3))
            def _():
                forward_all(npan - 1 - f)

            @pl.when(t == base + (1 if f == 0 else 4))
            def _():
                if f == 0:
                    t_load.wait()
                factor_panel(npan - 1 - f)

        w = t - lag

        @pl.when(jnp.logical_and(w >= 0, w < units))
        def _():
            phase, p, j, g = decode(w)
            chip = chip_at(g)
            for s in range(SUBS):
                at = pl.ds(s * piece, piece)
                arrived(1, w, s)

                @pl.when(centre)
                def _():
                    ab[1, w, at] = ab[1, w, at] + sbuf[w, at]

                @pl.when(jnp.logical_not(edge))
                def _():
                    outward(w, s).start()

                high, low = split(ab[1, w, at])
                sth[j, chip, at] = high
                stl[j, chip, at] = low

            @pl.when(g == nx - 1)
            def _():
                bh = sth[j].reshape(2 * kc * nx, cb)
                bl = stl[j].reshape(2 * kc * nx, cb)
                for r in range(0, rows, BLOCK):
                    at = pl.ds(r, BLOCK)
                    new = vbuf[j, at] - dot3(zh[p, at], zl[p, at], bh, bl, ((1,), (0,)))
                    vbuf[j, at] = new

                    @pl.when(phase < npan - 1)
                    def _():
                        high, low = split(vbuf[j, at])
                        vh[j, at] = high
                        vl[j, at] = low

                    @pl.when(phase == npan - 1)
                    def _():
                        out[at, pl.ds(pl.multiple_of(j * cb, cb), cb)] = vbuf[j, at]

        return carry

    lax.fori_loop(0, units + max_lag, step, 0)

    for p in range(npan):
        y_sib(p).wait_send()
        for g in range(1, nx):
            y_across(p, g).wait_send()
            y_forward(p, g).wait_send()

    def drain(u, carry):
        for s in range(SUBS):
            inward(u, s).wait_send()

            @pl.when(jnp.logical_not(edge))
            def _():
                outward(u, s).wait_send()

        return carry

    lax.fori_loop(0, units, drain, 0)


def per_device(nprow, npcol, eigvecs, y_panels, t_factors):
    rows, cols = eigvecs.shape
    npan, _, kc = y_panels.shape
    cb = BLOCK
    ncb = cols // cb
    nx = npcol // 2
    units = npan * ncb * nx
    dma = pltpu.SemaphoreType.DMA
    any_space = pl.BlockSpec(memory_space=pltpu.HBM)
    nb = kc * npcol
    return pl.pallas_call(
        functools.partial(kernel, rows, nprow, npcol),
        out_shape=jax.ShapeDtypeStruct((rows, cols), F32),
        in_specs=[any_space] * 3,
        out_specs=pl.BlockSpec(memory_space=pltpu.VMEM),
        scratch_shapes=[
            pltpu.VMEM((ncb, rows, cb), F32),
            pltpu.VMEM((ncb, rows, cb), BF16),
            pltpu.VMEM((ncb, rows, cb), BF16),
            pltpu.VMEM((npan, nx, 2, kc, rows), F32),
            pltpu.VMEM((npan, nx, 2, kc, rows), BF16),
            pltpu.VMEM((npan, nx, 2, kc, rows), BF16),
            pltpu.VMEM((npan, nb, nb), F32),
            pltpu.VMEM((npan, rows, nb), BF16),
            pltpu.VMEM((npan, rows, nb), BF16),
            pltpu.VMEM((units, 2 * kc, cb), F32),
            pltpu.VMEM((2, units, 2 * kc, cb), F32),
            pltpu.VMEM((ncb, nx, 2 * kc, cb), BF16),
            pltpu.VMEM((ncb, nx, 2 * kc, cb), BF16),
            dma((ncb,)),
            dma((npan,)),
            dma,
            dma((npan,)),
            dma((npan, nx - 1)),
            dma((npan, nx - 1)),
            dma((npan, nx, 2)),
            dma((units, SUBS)),
            dma((2, units, SUBS)),
            dma((units, SUBS)),
        ],
        compiler_params=pltpu.CompilerParams(
            collective_id=0, has_side_effects=True, vmem_limit_bytes=48 * 2**20
        ),
        cost_estimate=pl.CostEstimate(
            flops=2 * 3 * npan * rows * nb * (2 * cols + nb),
            bytes_accessed=8 * rows * cols,
            transcendentals=0,
        ),
    )(
        eigvecs,
        pltpu.with_memory_space_constraint(jnp.swapaxes(y_panels, 1, 2), pltpu.HBM),
        pltpu.with_memory_space_constraint(t_factors, pltpu.HBM),
    )


def solution(mesh):
    return jax.shard_map(
        functools.partial(per_device, mesh.shape["prow"], mesh.shape["pcol"]),
        mesh=mesh,
        in_specs=(
            P(("grp", "prow"), "pcol"),
            P(None, ("grp", "prow"), "pcol"),
            P("grp", None, None),
        ),
        out_specs=P(("grp", "prow"), "pcol"),
        check_vma=False,
    )
```

```python
import functools

import jax
import jax.numpy as jnp
from jax import lax
from jax.experimental import pallas as pl
from jax.experimental.pallas import tpu as pltpu
from jax.sharding import PartitionSpec as P

F32 = jnp.float32
BF16 = jnp.bfloat16
BLOCK = 256
SUBS = 2
LAG = 1
MESH = pl.DeviceIdType.MESH


def split(x):
    high = x.astype(BF16)
    return high, (x - high.astype(F32)).astype(BF16)


def dot3(ah, al, bh, bl, dims):
    dot = functools.partial(
        lax.dot_general, dimension_numbers=(dims, ((), ())), preferred_element_type=F32
    )
    return dot(ah, bh) + (dot(al, bh) + dot(ah, bl))


def kernel(
    rows, nprow, npcol,
    v_hbm, y_hbm, t_hbm, out,
    vbuf, vh, vl, yt, yth, ytl, tbuf, z3, sbuf, ab, st3,
    v_sem, y_sem, t_sem,
    ys_sem, yx_sem, yf_sem, yr_sem,
    in_send, in_recv, outw_send,
):
    npan = y_hbm.shape[0]
    kc = y_hbm.shape[1]
    ncb = vbuf.shape[0]
    nx = npcol // 2
    nb = kc * npcol
    per_phase = ncb * nx
    units = npan * per_phase
    piece = 2 * kc // SUBS
    cb = vbuf.shape[2]

    grp = lax.axis_index("grp")
    row = lax.axis_index("prow")
    col = lax.axis_index("pcol")
    x, core = col // 2, col % 2
    half = nprow // 2
    lower = row < half
    inner = jnp.where(lower, row + 1, row - 1)
    outer = jnp.where(lower, row - 1, row + 1)
    dist = jnp.where(lower, half - 1 - row, row - half)
    centre = dist == 0
    edge = dist == half - 1
    centre_slot = jnp.where(centre, 1, 0)
    lag_cap = min(
        [per_phase + j * nx - ((nx - 1) * (ncb - 1) + j) - 1 for j in range(ncb - 1)]
        + [(ncb - 1) * nx]
    )
    lag = jnp.minimum(LAG + 3 * dist, lag_cap)
    late = jnp.where(lag < lag_cap, 1, 0)
    max_lag = min(LAG + 3 * (half - 1), lag_cap)

    sibling = (grp, row, x * 2 + 1 - core)

    def across(g):
        return (grp, row, ((x + g) % nx) * 2 + core)

    def v_load(j):
        start = pl.multiple_of(j * cb, cb)
        return pltpu.make_async_copy(v_hbm.at[:, pl.ds(start, cb)], vbuf.at[j], v_sem.at[j])

    def y_load(p):
        return pltpu.make_async_copy(y_hbm.at[p], yt.at[p, x, core], y_sem.at[p])

    t_load = pltpu.make_async_copy(t_hbm, tbuf, t_sem)
    for p in reversed(range(npan)):
        y_load(p).start()
    for j in range(ncb):
        v_load(j).start()
    t_load.start()

    barrier = pltpu.get_barrier_semaphore()
    pl.semaphore_signal(barrier, inc=1, device_id=(grp, inner, col), device_id_type=MESH)

    @pl.when(jnp.logical_not(edge))
    def _():
        pl.semaphore_signal(barrier, inc=1, device_id=(grp, outer, col), device_id_type=MESH)

    pl.semaphore_signal(barrier, inc=1, device_id=sibling, device_id_type=MESH)
    for g in range(1, nx):
        pl.semaphore_signal(barrier, inc=1, device_id=across(g), device_id_type=MESH)

    for p in reversed(range(npan)):
        y_load(p).wait()
    pl.semaphore_wait(barrier, jnp.where(edge, 1, 2) + nx)

    def y_copy(p, chip, which, send_sem, target):
        return pltpu.make_async_remote_copy(
            src_ref=yt.at[p, chip, which],
            dst_ref=yt.at[p, chip, which],
            send_sem=send_sem,
            recv_sem=yr_sem.at[p, chip, which],
            device_id=target,
            device_id_type=MESH,
        )

    def y_sib(p):
        return y_copy(p, x, core, ys_sem.at[p], sibling)

    def y_across(p, g):
        return y_copy(p, x, core, yx_sem.at[p, g - 1], across(g))

    def chip_at(g):
        return (x + g) % nx

    def y_forward(p, g):
        return y_copy(p, chip_at(g), core, yf_sem.at[p, g - 1], sibling)

    def y_arrived(p, chip, which):
        y_copy(p, chip, which, ys_sem.at[p], sibling).wait_recv()

    def split_y(p, chip):
        for which in range(2):
            split_half(p, chip, which)

    def split_half(p, chip, which):
        high, low = split(yt[p, chip, which])
        yth[p, chip, which] = high
        ytl[p, chip, which] = low

    def forward_all(p):
        for g in range(1, nx):
            y_arrived(p, chip_at(g), core)
            y_forward(p, g).start()

    def finish_panel(p):
        for g in range(1, nx):
            y_arrived(p, chip_at(g), 1 - core)
            split_y(p, chip_at(g))

    def factor_panel(p):
        th, tl = split(tbuf[p])
        z = dot3(
            yth[p].reshape(2 * kc * nx, rows), ytl[p].reshape(2 * kc * nx, rows),
            th, tl, ((0,), (0,)),
        )
        high, low = split(z)
        for part, value in enumerate((high, low, high)):
            z3[p, :, pl.ds(part * nb, nb)] = value

    for p in reversed(range(npan)):
        y_sib(p).start()
        if p == npan - 1:
            for g in range(1, nx):
                y_across(p, g).start()
    split_half(npan - 1, x, core)

    def decode(u):
        phase = u // per_phase
        r = u % per_phase
        last = r >= (ncb - 1) * nx
        first = phase == 0
        j = jnp.where(first, jnp.where(last, ncb - 1, r % (ncb - 1)), r // nx)
        g = jnp.where(first, jnp.where(last, r - (ncb - 1) * nx, r // (ncb - 1)), r % nx)
        return phase, npan - 1 - phase, j, g

    def inward(u, s):
        at = pl.ds(s * piece, piece)
        return pltpu.make_async_remote_copy(
            src_ref=sbuf.at[u, at],
            dst_ref=ab.at[centre_slot, u, at],
            send_sem=in_send.at[u, s],
            recv_sem=in_recv.at[centre_slot, u, s],
            device_id=(grp, inner, col),
            device_id_type=MESH,
        )

    def outward(u, s):
        at = pl.ds(s * piece, piece)
        return pltpu.make_async_remote_copy(
            src_ref=ab.at[1, u, at],
            dst_ref=ab.at[1, u, at],
            send_sem=outw_send.at[u, s],
            recv_sem=in_recv.at[1, u, s],
            device_id=(grp, outer, col),
            device_id_type=MESH,
        )

    def arrived(slot, u, s):
        at = pl.ds(s * piece, piece)
        pltpu.make_async_remote_copy(
            src_ref=sbuf.at[u, at],
            dst_ref=ab.at[slot, u, at],
            send_sem=in_send.at[u, s],
            recv_sem=in_recv.at[slot, u, s],
            device_id=(grp, inner, col),
            device_id_type=MESH,
        ).wait_recv()

    def pass_inward(u, s):
        at = pl.ds(pl.multiple_of(s * piece, piece), piece)

        @pl.when(jnp.logical_not(edge))
        def _():
            arrived(0, u, s)
            sbuf[u, at] = sbuf[u, at] + ab[0, u, at]

        inward(u, s).start()

    begin = max(ncb - 2, 0)

    def update(w):
        phase, p, j, g = decode(w)

        @pl.when(g == nx - 1)
        def _():
            for r in range(0, rows, rows):
                at = pl.ds(r, rows)
                new = vbuf[j, at] - jnp.dot(
                        z3[p, at], st3[j].reshape(3 * nb, cb), preferred_element_type=F32
                    )
                vbuf[j, at] = new

                @pl.when(phase < npan - 1)
                def _():
                    high, low = split(vbuf[j, at])
                    vh[j, at] = high
                    vl[j, at] = low

                @pl.when(phase == npan - 1)
                def _():
                    out[at, pl.ds(pl.multiple_of(j * cb, cb), cb)] = vbuf[j, at]

    def step(t, carry):
        for f in range(npan):
            p = npan - 1 - f
            if f == 0:
                finish_at = begin + 1
            else:
                base = (f - 1) * per_phase + begin
                send_at, finish_at = base + 1, base + 4

                @pl.when(t == send_at)
                def _():
                    for g in range(1, nx):
                        y_across(p, g).start()

            @pl.when(t == finish_at)
            def _():
                if f > 0:
                    y_arrived(p, x, 1 - core)
                    split_y(p, x)
                finish_panel(p)

        @pl.when(t < units)
        def _():
            u = t
            phase, p, j, g = decode(u)

            @pl.when(jnp.logical_and(phase == 0, g == 0))
            def _():
                v_load(j).wait()
                high, low = split(vbuf[j])
                vh[j] = high
                vl[j] = low

            chip = chip_at(g)

            @pl.when(t == 0)
            def _():
                for turn, which in enumerate((core, 1 - core)):
                    if turn == 1:
                        y_arrived(p, x, which)
                        split_half(p, x, which)
                    sbuf[u, pl.ds(which * kc, kc)] = dot3(
                        yth[p, chip, which], ytl[p, chip, which], vh[j], vl[j], ((1,), (0,))
                    )
                    pass_inward(u, which)

            @pl.when(t > 0)
            def _():
                sbuf[u] = dot3(
                    yth[p, chip].reshape(2 * kc, rows), ytl[p, chip].reshape(2 * kc, rows),
                    vh[j], vl[j], ((1,), (0,)),
                )
                for s in range(SUBS):
                    pass_inward(u, s)

        for f in range(npan):
            base = max(f - 1, 0) * per_phase + begin

            @pl.when(t == base + (0 if f == 0 else 3))
            def _():
                forward_all(npan - 1 - f)

            @pl.when(t == base + (1 if f == 0 else 4))
            def _():
                if f == 0:
                    t_load.wait()
                factor_panel(npan - 1 - f)

        before = t - lag - 1

        @pl.when(jnp.logical_and(late == 1, jnp.logical_and(before >= 0, before < units)))
        def _():
            update(before)

        w = t - lag

        @pl.when(jnp.logical_and(w >= 0, w < units))
        def _():
            phase, p, j, g = decode(w)
            chip = chip_at(g)
            for s in range(SUBS):
                at = pl.ds(s * piece, piece)
                arrived(1, w, s)

                @pl.when(centre)
                def _():
                    ab[1, w, at] = ab[1, w, at] + sbuf[w, at]

                @pl.when(jnp.logical_not(edge))
                def _():
                    outward(w, s).start()

                high, low = split(ab[1, w, at])
                for part, value in enumerate((high, high, low)):
                    st3[j, part, chip, at] = value

        @pl.when(jnp.logical_and(late == 0, jnp.logical_and(w >= 0, w < units)))
        def _():
            update(w)

        return carry

    lax.fori_loop(0, units + max_lag + 1, step, 0)

    for p in range(npan):
        y_sib(p).wait_send()
        for g in range(1, nx):
            y_across(p, g).wait_send()
            y_forward(p, g).wait_send()

    def drain(u, carry):
        for s in range(SUBS):
            inward(u, s).wait_send()

            @pl.when(jnp.logical_not(edge))
            def _():
                outward(u, s).wait_send()

        return carry

    lax.fori_loop(0, units, drain, 0)


def per_device(nprow, npcol, eigvecs, y_panels, t_factors):
    rows, cols = eigvecs.shape
    npan, _, kc = y_panels.shape
    cb = BLOCK
    ncb = cols // cb
    nx = npcol // 2
    units = npan * ncb * nx
    dma = pltpu.SemaphoreType.DMA
    any_space = pl.BlockSpec(memory_space=pltpu.HBM)
    nb = kc * npcol
    return pl.pallas_call(
        functools.partial(kernel, rows, nprow, npcol),
        out_shape=jax.ShapeDtypeStruct((rows, cols), F32),
        in_specs=[any_space] * 3,
        out_specs=pl.BlockSpec(memory_space=pltpu.VMEM),
        scratch_shapes=[
            pltpu.VMEM((ncb, rows, cb), F32),
            pltpu.VMEM((ncb, rows, cb), BF16),
            pltpu.VMEM((ncb, rows, cb), BF16),
            pltpu.VMEM((npan, nx, 2, kc, rows), F32),
            pltpu.VMEM((npan, nx, 2, kc, rows), BF16),
            pltpu.VMEM((npan, nx, 2, kc, rows), BF16),
            pltpu.VMEM((npan, nb, nb), F32),
            pltpu.VMEM((npan, rows, 3 * nb), BF16),
            pltpu.VMEM((units, 2 * kc, cb), F32),
            pltpu.VMEM((2, units, 2 * kc, cb), F32),
            pltpu.VMEM((ncb, 3, nx, 2 * kc, cb), BF16),
            dma((ncb,)),
            dma((npan,)),
            dma,
            dma((npan,)),
            dma((npan, nx - 1)),
            dma((npan, nx - 1)),
            dma((npan, nx, 2)),
            dma((units, SUBS)),
            dma((2, units, SUBS)),
            dma((units, SUBS)),
        ],
        compiler_params=pltpu.CompilerParams(
            collective_id=0, has_side_effects=True, vmem_limit_bytes=48 * 2**20
        ),
        cost_estimate=pl.CostEstimate(
            flops=2 * 3 * npan * rows * nb * (2 * cols + nb),
            bytes_accessed=8 * rows * cols,
            transcendentals=0,
        ),
    )(
        eigvecs,
        pltpu.with_memory_space_constraint(jnp.swapaxes(y_panels, 1, 2), pltpu.HBM),
        pltpu.with_memory_space_constraint(t_factors, pltpu.HBM),
    )


def solution(mesh):
    return jax.shard_map(
        functools.partial(per_device, mesh.shape["prow"], mesh.shape["pcol"]),
        mesh=mesh,
        in_specs=(
            P(("grp", "prow"), "pcol"),
            P(None, ("grp", "prow"), "pcol"),
            P("grp", None, None),
        ),
        out_specs=P(("grp", "prow"), "pcol"),
        check_vma=False,
    )
```

```python
import functools

import jax
import jax.numpy as jnp
from jax import lax
from jax.experimental import pallas as pl
from jax.experimental.pallas import tpu as pltpu
from jax.sharding import PartitionSpec as P

F32 = jnp.float32
BF16 = jnp.bfloat16
BLOCK = 256
SUBS = 2
LAG = 1
MESH = pl.DeviceIdType.MESH


def split(x):
    high = x.astype(BF16)
    return high, (x - high.astype(F32)).astype(BF16)


def dot3(ah, al, bh, bl, dims):
    dot = functools.partial(
        lax.dot_general, dimension_numbers=(dims, ((), ())), preferred_element_type=F32
    )
    return dot(ah, bh) + (dot(al, bh) + dot(ah, bl))


def kernel(
    rows, nprow, npcol,
    v_hbm, y_hbm, t_hbm, out,
    vbuf, vh, vl, yt, yth, ytl, tbuf, z3, sbuf, ab, st3,
    v_sem, y_sem, t_sem,
    ys_sem, yx_sem, yf_sem, yr_sem,
    in_send, in_recv, outw_send,
):
    npan = y_hbm.shape[0]
    kc = y_hbm.shape[1]
    ncb = vbuf.shape[0]
    nx = npcol // 2
    nb = kc * npcol
    per_phase = ncb * nx
    units = npan * per_phase
    piece = 2 * kc // SUBS
    cb = vbuf.shape[2]

    grp = lax.axis_index("grp")
    row = lax.axis_index("prow")
    col = lax.axis_index("pcol")
    x, core = col // 2, col % 2
    half = nprow // 2
    lower = row < half
    inner = jnp.where(lower, row + 1, row - 1)
    outer = jnp.where(lower, row - 1, row + 1)
    dist = jnp.where(lower, half - 1 - row, row - half)
    centre = dist == 0
    edge = dist == half - 1
    centre_slot = jnp.where(centre, 1, 0)
    lag_cap = min(
        [per_phase + j * nx - ((nx - 1) * (ncb - 1) + j) - 1 for j in range(ncb - 1)]
        + [(ncb - 1) * nx]
    )
    lag = jnp.minimum(LAG + 3 * dist, lag_cap)
    late = jnp.where(lag < lag_cap, 1, 0)
    max_lag = min(LAG + 3 * (half - 1), lag_cap)

    sibling = (grp, row, x * 2 + 1 - core)

    def across(g):
        return (grp, row, ((x + g) % nx) * 2 + core)

    def v_load(j):
        start = pl.multiple_of(j * cb, cb)
        return pltpu.make_async_copy(v_hbm.at[:, pl.ds(start, cb)], vbuf.at[j], v_sem.at[j])

    def y_load(p):
        return pltpu.make_async_copy(y_hbm.at[p], yt.at[p, x, core], y_sem.at[p])

    t_load = pltpu.make_async_copy(t_hbm, tbuf, t_sem)
    for p in reversed(range(npan)):
        y_load(p).start()
    for j in range(ncb):
        v_load(j).start()
    t_load.start()

    barrier = pltpu.get_barrier_semaphore()
    pl.semaphore_signal(barrier, inc=1, device_id=(grp, inner, col), device_id_type=MESH)

    @pl.when(jnp.logical_not(edge))
    def _():
        pl.semaphore_signal(barrier, inc=1, device_id=(grp, outer, col), device_id_type=MESH)

    pl.semaphore_signal(barrier, inc=1, device_id=sibling, device_id_type=MESH)
    for g in range(1, nx):
        pl.semaphore_signal(barrier, inc=1, device_id=across(g), device_id_type=MESH)

    for p in reversed(range(npan)):
        y_load(p).wait()
    pl.semaphore_wait(barrier, jnp.where(edge, 1, 2) + nx)

    def y_copy(p, chip, which, send_sem, target):
        return pltpu.make_async_remote_copy(
            src_ref=yt.at[p, chip, which],
            dst_ref=yt.at[p, chip, which],
            send_sem=send_sem,
            recv_sem=yr_sem.at[p, chip, which],
            device_id=target,
            device_id_type=MESH,
        )

    def y_sib(p):
        return y_copy(p, x, core, ys_sem.at[p], sibling)

    def y_across(p, g):
        return y_copy(p, x, core, yx_sem.at[p, g - 1], across(g))

    def chip_at(g):
        return (x + g) % nx

    def y_forward(p, g):
        return y_copy(p, chip_at(g), core, yf_sem.at[p, g - 1], sibling)

    def y_arrived(p, chip, which):
        y_copy(p, chip, which, ys_sem.at[p], sibling).wait_recv()

    def split_y(p, chip):
        for which in range(2):
            split_half(p, chip, which)

    def split_half(p, chip, which):
        high, low = split(yt[p, chip, which])
        yth[p, chip, which] = high
        ytl[p, chip, which] = low

    def forward_all(p):
        for g in range(1, nx):
            y_arrived(p, chip_at(g), core)
            y_forward(p, g).start()

    def finish_panel(p):
        for g in range(1, nx):
            y_arrived(p, chip_at(g), 1 - core)
            split_y(p, chip_at(g))

    def factor_panel(p):
        th, tl = split(tbuf[p])
        z = dot3(
            yth[p].reshape(2 * kc * nx, rows), ytl[p].reshape(2 * kc * nx, rows),
            th, tl, ((0,), (0,)),
        )
        high, low = split(z)
        for part, value in enumerate((high, low, high)):
            z3[p, :, pl.ds(part * nb, nb)] = value

    for p in reversed(range(npan)):
        y_sib(p).start()
        if p == npan - 1:
            for g in range(1, nx):
                y_across(p, g).start()
    split_half(npan - 1, x, core)

    def decode(u):
        phase = u // per_phase
        r = u % per_phase
        last = r >= (ncb - 1) * nx
        first = phase == 0
        j = jnp.where(first, jnp.where(last, ncb - 1, r % (ncb - 1)), r // nx)
        g = jnp.where(first, jnp.where(last, r - (ncb - 1) * nx, r // (ncb - 1)), r % nx)
        return phase, npan - 1 - phase, j, g

    def inward(u, s):
        at = pl.ds(s * piece, piece)
        return pltpu.make_async_remote_copy(
            src_ref=sbuf.at[u, at],
            dst_ref=ab.at[centre_slot, u, at],
            send_sem=in_send.at[u, s],
            recv_sem=in_recv.at[centre_slot, u, s],
            device_id=(grp, inner, col),
            device_id_type=MESH,
        )

    def outward(u, s):
        at = pl.ds(s * piece, piece)
        return pltpu.make_async_remote_copy(
            src_ref=ab.at[1, u, at],
            dst_ref=ab.at[1, u, at],
            send_sem=outw_send.at[u, s],
            recv_sem=in_recv.at[1, u, s],
            device_id=(grp, outer, col),
            device_id_type=MESH,
        )

    def arrived(slot, u, s):
        at = pl.ds(s * piece, piece)
        pltpu.make_async_remote_copy(
            src_ref=sbuf.at[u, at],
            dst_ref=ab.at[slot, u, at],
            send_sem=in_send.at[u, s],
            recv_sem=in_recv.at[slot, u, s],
            device_id=(grp, inner, col),
            device_id_type=MESH,
        ).wait_recv()

    def pass_inward(u, s):
        at = pl.ds(pl.multiple_of(s * piece, piece), piece)

        @pl.when(jnp.logical_not(edge))
        def _():
            arrived(0, u, s)
            sbuf[u, at] = sbuf[u, at] + ab[0, u, at]

        inward(u, s).start()

    begin = max(ncb - 2, 0)

    def update(w):
        phase, p, j, g = decode(w)

        @pl.when(g == nx - 1)
        def _():
            def updated():
                return vbuf[j] - jnp.dot(
                    z3[p], st3[j].reshape(3 * nb, cb), preferred_element_type=F32
                )

            @pl.when(phase < npan - 1)
            def _():
                new = updated()
                vbuf[j] = new
                high, low = split(new)
                vh[j] = high
                vl[j] = low

            @pl.when(phase == npan - 1)
            def _():
                out[:, pl.ds(pl.multiple_of(j * cb, cb), cb)] = updated()

    def step(t, carry):
        for f in range(npan):
            p = npan - 1 - f
            if f == 0:
                finish_at = begin + 1
            else:
                base = (f - 1) * per_phase + begin
                send_at, finish_at = base + 1, base + 4

                @pl.when(t == send_at)
                def _():
                    for g in range(1, nx):
                        y_across(p, g).start()

            @pl.when(t == finish_at)
            def _():
                if f > 0:
                    y_arrived(p, x, 1 - core)
                    split_y(p, x)
                finish_panel(p)

        @pl.when(t < units)
        def _():
            u = t
            phase, p, j, g = decode(u)

            @pl.when(jnp.logical_and(phase == 0, g == 0))
            def _():
                v_load(j).wait()
                high, low = split(vbuf[j])
                vh[j] = high
                vl[j] = low

            chip = chip_at(g)

            @pl.when(t == 0)
            def _():
                for turn, which in enumerate((core, 1 - core)):
                    if turn == 1:
                        y_arrived(p, x, which)
                        split_half(p, x, which)
                    sbuf[u, pl.ds(which * kc, kc)] = dot3(
                        yth[p, chip, which], ytl[p, chip, which], vh[j], vl[j], ((1,), (0,))
                    )
                    pass_inward(u, which)

            @pl.when(t > 0)
            def _():
                sbuf[u] = dot3(
                    yth[p, chip].reshape(2 * kc, rows), ytl[p, chip].reshape(2 * kc, rows),
                    vh[j], vl[j], ((1,), (0,)),
                )
                for s in range(SUBS):
                    pass_inward(u, s)

        for f in range(npan):
            base = max(f - 1, 0) * per_phase + begin

            @pl.when(t == base + (0 if f == 0 else 3))
            def _():
                forward_all(npan - 1 - f)

            @pl.when(t == base + (1 if f == 0 else 4))
            def _():
                if f == 0:
                    t_load.wait()
                factor_panel(npan - 1 - f)

        before = t - lag - 1

        @pl.when(jnp.logical_and(late == 1, jnp.logical_and(before >= 0, before < units)))
        def _():
            update(before)

        w = t - lag

        @pl.when(jnp.logical_and(w >= 0, w < units))
        def _():
            phase, p, j, g = decode(w)
            chip = chip_at(g)
            for s in range(SUBS):
                at = pl.ds(s * piece, piece)
                arrived(1, w, s)

                @pl.when(centre)
                def _():
                    ab[1, w, at] = ab[1, w, at] + sbuf[w, at]

                @pl.when(jnp.logical_not(edge))
                def _():
                    outward(w, s).start()

                high, low = split(ab[1, w, at])
                for part, value in enumerate((high, high, low)):
                    st3[j, part, chip, at] = value

        @pl.when(jnp.logical_and(late == 0, jnp.logical_and(w >= 0, w < units)))
        def _():
            update(w)

        return carry

    lax.fori_loop(0, units + max_lag + 1, step, 0)

    for p in range(npan):
        y_sib(p).wait_send()
        for g in range(1, nx):
            y_across(p, g).wait_send()
            y_forward(p, g).wait_send()

    def drain(u, carry):
        for s in range(SUBS):
            inward(u, s).wait_send()

            @pl.when(jnp.logical_not(edge))
            def _():
                outward(u, s).wait_send()

        return carry

    lax.fori_loop(0, units, drain, 0)


def per_device(nprow, npcol, eigvecs, y_panels, t_factors):
    rows, cols = eigvecs.shape
    npan, _, kc = y_panels.shape
    cb = BLOCK
    ncb = cols // cb
    nx = npcol // 2
    units = npan * ncb * nx
    dma = pltpu.SemaphoreType.DMA
    any_space = pl.BlockSpec(memory_space=pltpu.HBM)
    nb = kc * npcol
    return pl.pallas_call(
        functools.partial(kernel, rows, nprow, npcol),
        out_shape=jax.ShapeDtypeStruct((rows, cols), F32),
        in_specs=[any_space] * 3,
        out_specs=pl.BlockSpec(memory_space=pltpu.VMEM),
        scratch_shapes=[
            pltpu.VMEM((ncb, rows, cb), F32),
            pltpu.VMEM((ncb, rows, cb), BF16),
            pltpu.VMEM((ncb, rows, cb), BF16),
            pltpu.VMEM((npan, nx, 2, kc, rows), F32),
            pltpu.VMEM((npan, nx, 2, kc, rows), BF16),
            pltpu.VMEM((npan, nx, 2, kc, rows), BF16),
            pltpu.VMEM((npan, nb, nb), F32),
            pltpu.VMEM((npan, rows, 3 * nb), BF16),
            pltpu.VMEM((units, 2 * kc, cb), F32),
            pltpu.VMEM((2, units, 2 * kc, cb), F32),
            pltpu.VMEM((ncb, 3, nx, 2 * kc, cb), BF16),
            dma((ncb,)),
            dma((npan,)),
            dma,
            dma((npan,)),
            dma((npan, nx - 1)),
            dma((npan, nx - 1)),
            dma((npan, nx, 2)),
            dma((units, SUBS)),
            dma((2, units, SUBS)),
            dma((units, SUBS)),
        ],
        compiler_params=pltpu.CompilerParams(
            collective_id=0, has_side_effects=True, vmem_limit_bytes=48 * 2**20
        ),
        cost_estimate=pl.CostEstimate(
            flops=2 * 3 * npan * rows * nb * (2 * cols + nb),
            bytes_accessed=8 * rows * cols,
            transcendentals=0,
        ),
    )(
        eigvecs,
        pltpu.with_memory_space_constraint(jnp.swapaxes(y_panels, 1, 2), pltpu.HBM),
        pltpu.with_memory_space_constraint(t_factors, pltpu.HBM),
    )


def solution(mesh):
    return jax.shard_map(
        functools.partial(per_device, mesh.shape["prow"], mesh.shape["pcol"]),
        mesh=mesh,
        in_specs=(
            P(("grp", "prow"), "pcol"),
            P(None, ("grp", "prow"), "pcol"),
            P("grp", None, None),
        ),
        out_specs=P(("grp", "prow"), "pcol"),
        check_vma=False,
    )
```
